32 devices in a mesh: grp: 2 (over y), beam: 4 (over z), slab: 2 (over x), pol: 2 (over core).
Axes of the slice: x: 2, y: 2, z: 4, core: 2. Of those that a mesh axis runs over, the one named last changes fastest.
Arguments:
- stokes: bfloat16 [2, 1024, 16384], P('pol', 'grp', ('beam', 'slab')), parts along dimension 1, may hold values from -6 to 6
- lambda_sq: float32 [16384], replicated, may hold values from 0.005 to 0.1
- channel_flags: int32 [16384], replicated, may hold values from 0 to 1, as said below
- counts: int32 [1024], P('grp'), parts along dimension 0, may hold values from 1 to 4
Outputs:
- spectrum: float32 [1024, 2048], P(('grp', 'beam', 'slab', 'pol')), parts along dimension 0
The draws below stay inside these ranges and needn't reach their ends.
There are 2 independent parts, one for each index of `grp`. The reference program is written for one: setup_inputs(seed, part) draws one part's arguments, and reference() takes and returns one part's arrays. A program takes and returns all parts, laid end to end along the dimension named above; an argument that names none is the same for every part. Nothing has to cross between parts.
Inputs may be any that keep to these rules, and one draw needn't show every extreme that they name: `channel_flags`: at least one channel is kept.
All inputs are finite; a program needn't handle non-finite values.
Results may differ from the reference program's by a relative error of at most 0.0032.
Values may be sent and summed in bfloat16 or wider, within the bound.
A program may use at most 64 MiB of HBM per device.

```python
import jax
import jax.numpy as jnp
from jax import lax

CHAN = 16384
NPHI = 1024
LEVELS = 4
DEPTH_BLOCK = 128
BEAMS = 512


def draw_counts(key, part):
    key = jax.random.fold_in(key, 11)
    keys = jax.random.split(key, 4)
    regions = 16
    region_of = jnp.arange(BEAMS, dtype=jnp.int32) * regions // BEAMS
    forced = jax.random.randint(keys[0], (), 0, regions)
    heavy = (jax.random.randint(keys[1], (regions,), 0, 4) == 0) | (jnp.arange(regions, dtype=jnp.int32) == forced)
    light_counts = jax.random.randint(keys[2], (BEAMS,), 1, 3)
    strong_counts = jax.random.randint(keys[3], (BEAMS,), LEVELS - 1, LEVELS + 1)
    heavy_rows = jnp.take(heavy, region_of)
    values = jnp.where(heavy_rows, strong_counts, light_counts)
    first_forced = forced * BEAMS // regions
    values = jnp.where(jnp.arange(BEAMS, dtype=jnp.int32) == first_forced, LEVELS, values)
    return values.astype(jnp.int32)


def draw_channel_flags(key, part):
    key = jax.random.fold_in(key, 23)
    keys = jax.random.split(key, 2)
    draws = jax.random.randint(keys[0], (CHAN,), 0, 8)
    kept = jax.random.randint(keys[1], (), 0, CHAN)
    chosen = (draws > 0) | (jnp.arange(CHAN, dtype=jnp.int32) == kept)
    return jnp.where(chosen, 1, 0).astype(jnp.int32)


def block_scale(rng, extent, cuts, smallest, largest):
    def one(axis_at, parts):
        steps = jax.random.uniform(jax.random.fold_in(jax.random.fold_in(rng, 6), axis_at), (parts,), jnp.float32, smallest / len(cuts), largest / len(cuts))
        return jnp.repeat(jnp.exp(steps), extent[axis_at] // parts).reshape((-1,) + (1,) * (len(extent) - axis_at - 1))

    factor_of = one(*cuts[0])
    for cut in cuts[1:]:
        factor_of = factor_of * one(*cut)
    return factor_of


def normal_values(key, shape, width, limit, pieces=(), held_as=jnp.bfloat16):
    entries = width * jax.random.normal(key, shape, jnp.float32)
    if pieces:
        entries = entries * block_scale(key, shape, pieces, -0.22, 0.18)
    return jnp.clip(entries, -limit, limit).astype(held_as)


def setup_inputs(seed: int = 0, part: int = 0) -> dict:
    streams_of = jax.random.split(jax.random.key(seed), 5)
    part_splits = jax.random.split(jax.random.fold_in(streams_of[4], part), 5)
    stokes = normal_values(part_splits[0], (2, BEAMS, CHAN), 1.0, 6.0, ((0, 2), (2, 8)))
    lambda_sq = jnp.clip(jax.random.uniform(streams_of[1], (CHAN,), jnp.float32, 0.005, 0.1), 0.005, 0.1)
    channel_flags = draw_channel_flags(jax.random.fold_in(streams_of[4], 71), part)
    counts = draw_counts(jax.random.fold_in(jax.random.fold_in(streams_of[4], part), 71), part)
    return dict(stokes=stokes, lambda_sq=lambda_sq, channel_flags=channel_flags, counts=counts)


depth_step = 32.0

def build_tables(lambda_block, flag_block, norm_scale, center):
    depths = depth_step * (jnp.arange(NPHI, dtype=jnp.int32).astype(jnp.float32) - NPHI // 2)
    phases = (2.0 * depths)[None, :] * (lambda_block - center)[:, None]
    weight = (norm_scale * flag_block)[:, None]
    cos_table = (weight * jnp.cos(phases)).astype(jnp.bfloat16)
    sin_table = (weight * jnp.sin(phases)).astype(jnp.bfloat16)
    return (cos_table, sin_table)

def reference(stokes, lambda_sq, channel_flags, counts):
    flag_float = channel_flags.astype(jnp.float32)
    flag_total = jnp.sum(flag_float)
    norm_scale = 1.0 / jnp.sqrt(flag_total)
    center = jnp.sum(flag_float * lambda_sq) / flag_total
    block_width = min(2048, CHAN)
    block_count = CHAN // block_width
    stokes_q = stokes[0]
    stokes_u = stokes[1]

    def add_block(totals, index):
        offset = (index * block_width).astype(jnp.int32)
        q_block = lax.dynamic_slice_in_dim(stokes_q, offset, block_width, 1)
        u_block = lax.dynamic_slice_in_dim(stokes_u, offset, block_width, 1)
        lambda_block = lax.dynamic_slice_in_dim(lambda_sq, offset, block_width, 0)
        flag_block = lax.dynamic_slice_in_dim(flag_float, offset, block_width, 0)
        cos_table, sin_table = build_tables(lambda_block, flag_block, norm_scale, center)
        real_part = jnp.dot(q_block, cos_table, preferred_element_type=jnp.float32) + jnp.dot(u_block, sin_table, preferred_element_type=jnp.float32)
        imag_part = jnp.dot(u_block, cos_table, preferred_element_type=jnp.float32) - jnp.dot(q_block, sin_table, preferred_element_type=jnp.float32)
        return (totals + jnp.concatenate([real_part, imag_part], 1), None)
    start_totals = jnp.zeros((BEAMS, 2 * NPHI), jnp.float32)
    totals, unused = lax.scan(add_block, start_totals, jnp.arange(block_count, dtype=jnp.int32))
    depth_ids = jnp.arange(NPHI, dtype=jnp.int32)
    middle = NPHI // 2
    lower = middle - DEPTH_BLOCK * counts
    upper = middle + DEPTH_BLOCK * counts
    inside = (depth_ids[None, :] >= lower[:, None]) & (depth_ids[None, :] < upper[:, None])
    keep_mask = jnp.concatenate([inside, inside], 1)
    return jnp.where(keep_mask, totals, jnp.zeros_like(totals))
```

```python
import functools
import math

import jax
import jax.numpy as jnp
from jax import lax
from jax.experimental import pallas as pl
from jax.experimental.pallas import tpu as pltpu
from jax.sharding import PartitionSpec as P

NPHI = 1024
DEPTH_BLOCK = 128
MESH = pl.DeviceIdType.MESH


depth_step = 32.0


def depth_values(depth_ids):
    return depth_step * (depth_ids.astype(jnp.float32) - NPHI // 2)


def build_table(lambda_block, flag_block, norm_scale, center, depths, first_pol):
    phases = (2.0 * depths)[None, :] * (lambda_block - center)[:, None]
    weight = (norm_scale * flag_block)[:, None]
    cos_part = weight * jnp.cos(phases)
    sin_part = weight * jnp.sin(phases)
    first_table = jnp.where(first_pol, cos_part, sin_part).astype(jnp.bfloat16)
    second_table = jnp.where(first_pol, -sin_part, cos_part).astype(jnp.bfloat16)
    return jnp.concatenate([first_table, second_table], 1)


def synth_dense(turned, lambda_local, flag_local, norm_scale, center, first_pol):
    row_count, chan_count = turned.shape
    block_width = min(1024, chan_count)
    block_count = chan_count // block_width
    depths = depth_values(jnp.arange(NPHI, dtype=jnp.int32))

    def add_block(index, totals):
        offset = index * block_width
        block = lax.dynamic_slice_in_dim(turned, offset, block_width, 1)
        lambda_block = lax.dynamic_slice_in_dim(lambda_local, offset, block_width, 0)
        flag_block = lax.dynamic_slice_in_dim(flag_local, offset, block_width, 0)
        phase_table = build_table(lambda_block, flag_block, norm_scale, center, depths, first_pol)
        return totals + jnp.dot(block, phase_table, preferred_element_type=jnp.float32)

    start_totals = jnp.zeros((row_count, 2 * NPHI), jnp.float32)
    return lax.fori_loop(0, block_count, add_block, start_totals)


def depth_mask(row_counts):
    depth_ids = jnp.arange(NPHI, dtype=jnp.int32)
    middle = NPHI // 2
    lower = middle - DEPTH_BLOCK * row_counts
    upper = middle + DEPTH_BLOCK * row_counts
    inside = (depth_ids[None, :] >= lower[:, None]) & (depth_ids[None, :] < upper[:, None])
    return jnp.concatenate([inside, inside], 1)


def general_shards(stokes, lambda_sq, channel_flags, counts):
    local_stokes = stokes[0]
    flag_float = channel_flags.astype(jnp.float32)
    flag_total = jnp.sum(flag_float)
    norm_scale = 1.0 / jnp.sqrt(flag_total)
    center = jnp.sum(flag_float * lambda_sq) / flag_total
    first_pol = lax.axis_index("pol") == 0
    beam_count = lax.axis_size("beam")
    slab_count = lax.axis_size("slab")
    total_beams = counts.shape[0]
    piece_index = lax.axis_index("beam")
    piece_rows = total_beams // beam_count
    turned = lax.all_to_all(local_stokes, "beam", split_axis=0, concat_axis=1, tiled=True)
    slab_index = lax.axis_index("slab")
    lambda_local = lax.dynamic_index_in_dim(
        lambda_sq.reshape(beam_count, slab_count, -1), slab_index, 1, keepdims=False
    ).reshape(-1)
    flag_local = lax.dynamic_index_in_dim(
        flag_float.reshape(beam_count, slab_count, -1), slab_index, 1, keepdims=False
    ).reshape(-1)
    row_counts = lax.dynamic_slice_in_dim(counts, piece_index * piece_rows, piece_rows, 0)
    partial_value = synth_dense(turned, lambda_local, flag_local, norm_scale, center, first_pol)
    partial_value = jnp.where(depth_mask(row_counts), partial_value, jnp.zeros_like(partial_value))
    return lax.psum_scatter(partial_value, ("slab", "pol"), scatter_dimension=0, tiled=True)


LANES = 128
PORTIONS = 4
COLS = NPHI // PORTIONS
FINE = 64
COARSE = NPHI // FINE

HALF_TURN_HI = 3.140625
HALF_TURN_MID = 9.670257568359375e-04
HALF_TURN_LO = math.pi - HALF_TURN_HI - HALF_TURN_MID


def cos_sin(phase):
    turns = jnp.floor(phase * (1.0 / math.pi) + 0.5)
    rest = phase - turns * HALF_TURN_HI
    rest = rest - turns * HALF_TURN_MID
    rest = rest - turns * HALF_TURN_LO
    sign = 1.0 - 2.0 * (turns - 2.0 * jnp.floor(turns * 0.5))
    square = rest * rest
    cos_sum = jnp.full_like(square, 1.0 / math.factorial(12))
    for order in (10, 8, 6, 4, 2, 0):
        cos_sum = cos_sum * square + (-1.0) ** (order // 2) / math.factorial(order)
    sin_sum = jnp.full_like(square, -1.0 / math.factorial(11))
    for order in (9, 7, 5, 3, 1):
        sin_sum = sin_sum * square + (-1.0) ** (order // 2) / math.factorial(order)
    return sign * cos_sum, sign * rest * sin_sum


def kernel(nz, nx, rows, chans,
           stokes_ref, lam_ref, flag_ref, out_ref,
           data, fine, coarse, table, sums, xout, xin, zout, zin,
           local_sem, pol_send, pol_recv, x_send, x_recv, z_send, z_recv):
    z = lax.axis_index("beam")
    x = lax.axis_index("slab")
    p = lax.axis_index("pol")
    groups = chans // LANES

    barrier = pltpu.get_barrier_semaphore()
    pl.semaphore_signal(barrier, inc=1, device_id={"pol": 1 - p}, device_id_type=MESH)
    pl.semaphore_signal(barrier, inc=1, device_id={"slab": 1 - x}, device_id_type=MESH)

    @pl.when(z > 0)
    def _():
        pl.semaphore_signal(barrier, inc=1, device_id={"beam": z - 1}, device_id_type=MESH)

    @pl.when(z < nz - 1)
    def _():
        pl.semaphore_signal(barrier, inc=1, device_id={"beam": z + 1}, device_id_type=MESH)

    def local_copy(xd):
        return pltpu.make_async_copy(stokes_ref.at[:, xd, p], data.at[0, xd], local_sem.at[xd])

    def pol_copy(xd):
        return pltpu.make_async_remote_copy(
            src_ref=stokes_ref.at[:, xd, 1 - p], dst_ref=data.at[1, xd],
            send_sem=pol_send.at[xd], recv_sem=pol_recv.at[xd],
            device_id={"pol": 1 - p}, device_id_type=MESH)

    def x_copy(j):
        return pltpu.make_async_remote_copy(
            src_ref=xout.at[j], dst_ref=xin.at[j],
            send_sem=x_send.at[j], recv_sem=x_recv.at[j],
            device_id={"slab": 1 - x}, device_id_type=MESH)

    def z_copy(j, d, way):
        return pltpu.make_async_remote_copy(
            src_ref=zout.at[j, d], dst_ref=zin.at[j, d, way],
            send_sem=z_send.at[j, d], recv_sem=z_recv.at[j, d, way],
            device_id={"beam": z + 1 - 2 * way}, device_id_type=MESH)

    for xd in range(nx):
        local_copy(xd).start()

    at_end = (z == 0) | (z == nz - 1)

    @pl.when(at_end)
    def _():
        pl.semaphore_wait(barrier, 3)

    @pl.when(jnp.logical_not(at_end))
    def _():
        pl.semaphore_wait(barrier, 4)

    for xd in range(nx):
        pol_copy(xd).start()

    flags = flag_ref[...].astype(jnp.float32)
    flag_total = jnp.sum(jnp.sum(flags, 0, keepdims=True), 1, keepdims=True)
    lam_total = jnp.sum(jnp.sum(flags * lam_ref[...], 0, keepdims=True), 1, keepdims=True)
    norm_scale = 1.0 / jnp.sqrt(flag_total)
    center = lam_total / flag_total
    first_group = (z * nx + x) * groups
    row_id = lax.broadcasted_iota(jnp.int32, (8, LANES), 0).astype(jnp.float32)
    step = 2.0 * depth_step

    def factors(g, carry):
        lanes = pl.ds(pl.multiple_of(g * LANES, LANES), LANES)
        offset = lam_ref[pl.ds(first_group + g, 1), :] - center
        weight = norm_scale * flag_ref[pl.ds(first_group + g, 1), :].astype(jnp.float32)
        cos_c, sin_c = cos_sin((step * row_id) * offset)
        cos_b, sin_b = cos_sin((step * 8.0 * row_id) * offset)
        for b in range(8):
            cb, sb = cos_b[b:b + 1, :], sin_b[b:b + 1, :]
            fine[0, b * 8:b * 8 + 8, lanes] = cb * cos_c - sb * sin_c
            fine[1, b * 8:b * 8 + 8, lanes] = sb * cos_c + cb * sin_c
        for half in range(COARSE // 8):
            ca, sa = cos_sin((step * FINE * (row_id + (8.0 * half - COARSE // 2))) * offset)
            coarse[0, half * 8:half * 8 + 8, lanes] = ca * weight
            coarse[1, half * 8:half * 8 + 8, lanes] = sa * weight
        return carry

    lax.fori_loop(0, groups, factors, 0)

    for xd in range(nx):
        local_copy(xd).wait()
        pol_copy(xd).wait()

    width = 256

    def compute(j):
        def fill(i, carry):
            a = i // (chans // width)
            lanes = pl.ds(pl.multiple_of((i % (chans // width)) * width, width), width)
            out_rows = pl.ds(pl.multiple_of(a * FINE, FINE), FINE)
            ca = coarse[0, pl.ds(j * (COLS // FINE) + a, 1), lanes]
            sa = coarse[1, pl.ds(j * (COLS // FINE) + a, 1), lanes]
            cf = fine[0, :, lanes]
            sf = fine[1, :, lanes]
            table[p, out_rows, lanes] = (ca * cf - sa * sf).astype(jnp.bfloat16)
            table[1 - p, out_rows, lanes] = (sa * cf + ca * sf).astype(jnp.bfloat16)
            return carry

        lax.fori_loop(0, (COLS // FINE) * (chans // width), fill, 0)
        sign = 1.0 - 2.0 * p.astype(jnp.float32)
        dims = (((1,), (1,)), ((), ()))
        half_rows = nz * rows

        def half(i, carry):
            xd = lax.rem(1 - x + i + nx, nx)
            both = data[:, xd].reshape(2 * half_rows, chans)
            first = lax.dot_general(both, table[0], dims, preferred_element_type=jnp.float32)
            second = lax.dot_general(both, table[1], dims, preferred_element_type=jnp.float32)
            real = first[:half_rows] + second[half_rows:]
            imag = sign * (first[half_rows:] - second[:half_rows])

            @pl.when(i == 0)
            def _():
                xout[j, 0] = real.astype(jnp.bfloat16)
                xout[j, 1] = imag.astype(jnp.bfloat16)
                x_copy(j).start()

            @pl.when(i == 1)
            def _():
                sums[j, 0] = real
                sums[j, 1] = imag

            return carry

        lax.fori_loop(0, nx, half, 0)

    def block(d):
        return slice(d * rows, d * rows + rows)

    def send(j, d, way, came):
        value = sums[j, :, block(d), :]
        if came:
            value = value + zin[j, d, way].astype(jnp.float32)
        zout[j, d] = value.astype(jnp.bfloat16)
        z_copy(j, d, way).start()

    def after_x(j):
        x_copy(j).wait_recv()
        sums[j] = sums[j] + xin[j].astype(jnp.float32)

        @pl.when(z == 0)
        def _():
            for d in range(nz - 1, 0, -1):
                send(j, d, 0, False)

        @pl.when(z == nz - 1)
        def _():
            for d in range(nz - 1):
                send(j, d, 1, False)

    def hop(j, h):
        for d in range(nz - 1, h, -1):
            @pl.when(z == h)
            def _():
                z_copy(j, d, 0).wait_recv()
                send(j, d, 0, True)

        for d in range(nz - 1 - h):
            @pl.when(z == nz - 1 - h)
            def _():
                z_copy(j, d, 1).wait_recv()
                send(j, d, 1, True)

    def finish(j):
        for d in range(nz):
            @pl.when(z == d)
            def _():
                value = sums[j, :, block(d), :]
                if d > 0:
                    z_copy(j, d, 0).wait_recv()
                    value = value + zin[j, d, 0].astype(jnp.float32)
                if d < nz - 1:
                    z_copy(j, d, 1).wait_recv()
                    value = value + zin[j, d, 1].astype(jnp.float32)
                for part in range(2):
                    columns = pl.ds(pl.multiple_of(part * NPHI + j * COLS, COLS), COLS)
                    out_ref[:, columns] = value[part]

    def stage(i, carry):
        @pl.when(i < PORTIONS)
        def _():
            compute(i)

        def late(lag, action):
            @pl.when((i >= lag) & (i < PORTIONS + lag))
            def _():
                action(i - lag)

        late(1, after_x)
        for h in range(1, nz - 1):
            late(1 + h, lambda j, h=h: hop(j, h))
        late(nz, finish)
        return carry

    lax.fori_loop(0, PORTIONS + nz, stage, 0)

    def drain(j, carry):
        x_copy(j).wait_send()
        for d in range(nz):
            @pl.when(z < d)
            def _():
                z_copy(j, d, 0).wait_send()

            @pl.when(z > d)
            def _():
                z_copy(j, d, 1).wait_send()
        return carry

    lax.fori_loop(0, PORTIONS, drain, 0)


def kernel_shards(nz, nx, stokes, lambda_sq, channel_flags, counts):
    beams = counts.shape[0]
    chans = stokes.shape[2]
    rows = beams // (nz * nx * 2)
    bf16, f32 = jnp.bfloat16, jnp.float32
    DMA = pltpu.SemaphoreType.DMA
    spectrum = pl.pallas_call(
        functools.partial(kernel, nz, nx, rows, chans),
        out_shape=jax.ShapeDtypeStruct((rows, 2 * NPHI), f32),
        in_specs=[
            pl.BlockSpec(memory_space=pl.ANY),
            pl.BlockSpec(memory_space=pltpu.VMEM),
            pl.BlockSpec(memory_space=pltpu.VMEM),
        ],
        out_specs=pl.BlockSpec(memory_space=pltpu.VMEM),
        scratch_shapes=[
            pltpu.VMEM((2, nx, nz, rows, chans), bf16),
            pltpu.VMEM((2, FINE, chans), f32),
            pltpu.VMEM((2, COARSE, chans), f32),
            pltpu.VMEM((2, COLS, chans), bf16),
            pltpu.VMEM((PORTIONS, 2, nz * rows, COLS), f32),
            pltpu.VMEM((PORTIONS, 2, nz * rows, COLS), bf16),
            pltpu.VMEM((PORTIONS, 2, nz * rows, COLS), bf16),
            pltpu.VMEM((PORTIONS, nz, 2, rows, COLS), bf16),
            pltpu.VMEM((PORTIONS, nz, 2, 2, rows, COLS), bf16),
            DMA((nx,)), DMA((nx,)), DMA((nx,)),
            DMA((PORTIONS,)), DMA((PORTIONS,)),
            DMA((PORTIONS, nz)), DMA((PORTIONS, nz, 2)),
        ],
        compiler_params=pltpu.CompilerParams(
            collective_id=0, has_side_effects=True, vmem_limit_bytes=40 * 2**20),
        cost_estimate=pl.CostEstimate(
            flops=4 * beams * chans * NPHI, bytes_accessed=2 * beams * chans, transcendentals=0),
    )(
        stokes.reshape(nz, nx, 2, rows, chans),
        lambda_sq.reshape(-1, LANES),
        channel_flags.reshape(-1, LANES),
    )
    owner = (lax.axis_index("beam") * nx + lax.axis_index("slab")) * 2 + lax.axis_index("pol")
    row_counts = lax.dynamic_slice_in_dim(counts, owner * rows, rows, 0)
    return jnp.where(depth_mask(row_counts), spectrum, jnp.zeros_like(spectrum))


def solution(mesh):
    in_specs = (P("pol", "grp", ("beam", "slab")), P(), P(), P("grp"))
    out_specs = P(("grp", "beam", "slab", "pol"), None)
    nz, nx = mesh.shape["beam"], mesh.shape["slab"]
    if nx == 2 and 2 <= nz <= 4 and mesh.shape["pol"] == 2:
        body = functools.partial(kernel_shards, nz, nx)
    else:
        body = general_shards
    return jax.shard_map(body, mesh=mesh, in_specs=in_specs, out_specs=out_specs, check_vma=False)
```

```python
import functools
import math

import jax
import jax.numpy as jnp
from jax import lax
from jax.experimental import pallas as pl
from jax.experimental.pallas import tpu as pltpu
from jax.sharding import PartitionSpec as P

NPHI = 1024
DEPTH_BLOCK = 128
MESH = pl.DeviceIdType.MESH


depth_step = 32.0


def depth_values(depth_ids):
    return depth_step * (depth_ids.astype(jnp.float32) - NPHI // 2)


def build_table(lambda_block, flag_block, norm_scale, center, depths, first_pol):
    phases = (2.0 * depths)[None, :] * (lambda_block - center)[:, None]
    weight = (norm_scale * flag_block)[:, None]
    cos_part = weight * jnp.cos(phases)
    sin_part = weight * jnp.sin(phases)
    first_table = jnp.where(first_pol, cos_part, sin_part).astype(jnp.bfloat16)
    second_table = jnp.where(first_pol, -sin_part, cos_part).astype(jnp.bfloat16)
    return jnp.concatenate([first_table, second_table], 1)


def synth_dense(turned, lambda_local, flag_local, norm_scale, center, first_pol):
    row_count, chan_count = turned.shape
    block_width = min(1024, chan_count)
    block_count = chan_count // block_width
    depths = depth_values(jnp.arange(NPHI, dtype=jnp.int32))

    def add_block(index, totals):
        offset = index * block_width
        block = lax.dynamic_slice_in_dim(turned, offset, block_width, 1)
        lambda_block = lax.dynamic_slice_in_dim(lambda_local, offset, block_width, 0)
        flag_block = lax.dynamic_slice_in_dim(flag_local, offset, block_width, 0)
        phase_table = build_table(lambda_block, flag_block, norm_scale, center, depths, first_pol)
        return totals + jnp.dot(block, phase_table, preferred_element_type=jnp.float32)

    start_totals = jnp.zeros((row_count, 2 * NPHI), jnp.float32)
    return lax.fori_loop(0, block_count, add_block, start_totals)


def depth_mask(row_counts):
    depth_ids = jnp.arange(NPHI, dtype=jnp.int32)
    middle = NPHI // 2
    lower = middle - DEPTH_BLOCK * row_counts
    upper = middle + DEPTH_BLOCK * row_counts
    inside = (depth_ids[None, :] >= lower[:, None]) & (depth_ids[None, :] < upper[:, None])
    return jnp.concatenate([inside, inside], 1)


def general_shards(stokes, lambda_sq, channel_flags, counts):
    local_stokes = stokes[0]
    flag_float = channel_flags.astype(jnp.float32)
    flag_total = jnp.sum(flag_float)
    norm_scale = 1.0 / jnp.sqrt(flag_total)
    center = jnp.sum(flag_float * lambda_sq) / flag_total
    first_pol = lax.axis_index("pol") == 0
    beam_count = lax.axis_size("beam")
    slab_count = lax.axis_size("slab")
    total_beams = counts.shape[0]
    piece_index = lax.axis_index("beam")
    piece_rows = total_beams // beam_count
    turned = lax.all_to_all(local_stokes, "beam", split_axis=0, concat_axis=1, tiled=True)
    slab_index = lax.axis_index("slab")
    lambda_local = lax.dynamic_index_in_dim(
        lambda_sq.reshape(beam_count, slab_count, -1), slab_index, 1, keepdims=False
    ).reshape(-1)
    flag_local = lax.dynamic_index_in_dim(
        flag_float.reshape(beam_count, slab_count, -1), slab_index, 1, keepdims=False
    ).reshape(-1)
    row_counts = lax.dynamic_slice_in_dim(counts, piece_index * piece_rows, piece_rows, 0)
    partial_value = synth_dense(turned, lambda_local, flag_local, norm_scale, center, first_pol)
    partial_value = jnp.where(depth_mask(row_counts), partial_value, jnp.zeros_like(partial_value))
    return lax.psum_scatter(partial_value, ("slab", "pol"), scatter_dimension=0, tiled=True)


LANES = 128
PORTIONS = 4
COLS = NPHI // PORTIONS
FINE = 64
COARSE = NPHI // FINE

VMEM_BYTES = 60 * 2**20

HALF_TURN_HI = 3.140625
HALF_TURN_MID = 9.670257568359375e-04
HALF_TURN_LO = math.pi - HALF_TURN_HI - HALF_TURN_MID


def cos_sin(phase):
    turns = jnp.floor(phase * (1.0 / math.pi) + 0.5)
    rest = phase - turns * HALF_TURN_HI
    rest = rest - turns * HALF_TURN_MID
    rest = rest - turns * HALF_TURN_LO
    sign = 1.0 - 2.0 * (turns - 2.0 * jnp.floor(turns * 0.5))
    square = rest * rest
    cos_sum = jnp.full_like(square, 1.0 / math.factorial(12))
    for order in (10, 8, 6, 4, 2, 0):
        cos_sum = cos_sum * square + (-1.0) ** (order // 2) / math.factorial(order)
    sin_sum = jnp.full_like(square, -1.0 / math.factorial(11))
    for order in (9, 7, 5, 3, 1):
        sin_sum = sin_sum * square + (-1.0) ** (order // 2) / math.factorial(order)
    return sign * cos_sum, sign * rest * sin_sum


def kernel(nz, nx, rows, chans,
           stokes_ref, lam_hbm, flag_hbm, count_hbm, out_ref,
           lam_ref, flag_ref, count_ref,
           data, fine, coarse, table, sums, xout, xin, zout, zin,
           small_sem, local_sem, pol_send, pol_recv, x_send, x_recv, z_send, z_recv):
    z = lax.axis_index("beam")
    x = lax.axis_index("slab")
    p = lax.axis_index("pol")
    groups = chans // LANES

    side = z // 2
    outer = (z == 0) | (z == nz - 1)
    near_in, near_out = 1 + side, 3 * side
    far_in, far_out = 2 - side, 3 - 3 * side

    barrier = pltpu.get_barrier_semaphore()

    def greet(**device):
        pl.semaphore_signal(barrier, inc=1, device_id=device, device_id_type=MESH)

    greet(pol=1 - p)
    greet(slab=1 - x)
    greet(beam=far_in)

    @pl.when(outer)
    def _():
        greet(beam=near_in)

    @pl.when(jnp.logical_not(outer))
    def _():
        greet(beam=near_out)
        greet(beam=far_out)

    def local_copy(xd):
        return pltpu.make_async_copy(stokes_ref.at[:, xd, p], data.at[0, xd], local_sem.at[xd])

    def pol_copy(xd):
        return pltpu.make_async_remote_copy(
            src_ref=stokes_ref.at[:, xd, 1 - p], dst_ref=data.at[1, xd],
            send_sem=pol_send.at[xd], recv_sem=pol_recv.at[xd],
            device_id={"pol": 1 - p}, device_id_type=MESH)

    def x_copy(j):
        return pltpu.make_async_remote_copy(
            src_ref=xout.at[j], dst_ref=xin.at[j],
            send_sem=x_send.at[j], recv_sem=x_recv.at[j],
            device_id={"slab": 1 - x}, device_id_type=MESH)

    def z_copy(j, taken, slot, to):
        return pltpu.make_async_remote_copy(
            src_ref=zout.at[j, taken], dst_ref=zin.at[j, slot],
            send_sem=z_send.at[j, taken], recv_sem=z_recv.at[j, slot],
            device_id={"beam": to}, device_id_type=MESH)

    small = [pltpu.make_async_copy(source, held, small_sem.at[i]) for i, (source, held) in enumerate(
        [(lam_hbm, lam_ref), (flag_hbm, flag_ref), (count_hbm, count_ref)])]
    for copy in small:
        copy.start()
    for xd in range(nx):
        local_copy(xd).start()

    @pl.when(outer)
    def _():
        pl.semaphore_wait(barrier, 4)

    @pl.when(jnp.logical_not(outer))
    def _():
        pl.semaphore_wait(barrier, 5)

    for xd in range(nx):
        pol_copy(xd).start()

    for copy in small:
        copy.wait()
    flags = flag_ref[...].astype(jnp.float32)
    flag_total = jnp.sum(jnp.sum(flags, 0, keepdims=True), 1, keepdims=True)
    lam_total = jnp.sum(jnp.sum(flags * lam_ref[...], 0, keepdims=True), 1, keepdims=True)
    norm_scale = 1.0 / jnp.sqrt(flag_total)
    center = lam_total / flag_total
    first_group = (z * nx + x) * groups
    row_id = lax.broadcasted_iota(jnp.int32, (8, LANES), 0).astype(jnp.float32)
    step = 2.0 * depth_step

    def factors(g, carry):
        lanes = pl.ds(pl.multiple_of(g * LANES, LANES), LANES)
        offset = lam_ref[pl.ds(first_group + g, 1), :] - center
        weight = norm_scale * flag_ref[pl.ds(first_group + g, 1), :].astype(jnp.float32)
        cos_c, sin_c = cos_sin((step * row_id) * offset)
        cos_b, sin_b = cos_sin((step * 8.0 * row_id) * offset)
        for b in range(8):
            cb, sb = cos_b[b:b + 1, :], sin_b[b:b + 1, :]
            fine[0, b * 8:b * 8 + 8, lanes] = cb * cos_c - sb * sin_c
            fine[1, b * 8:b * 8 + 8, lanes] = sb * cos_c + cb * sin_c
        for half in range(COARSE // 8):
            ca, sa = cos_sin((step * FINE * (row_id + (8.0 * half - COARSE // 2))) * offset)
            coarse[0, half * 8:half * 8 + 8, lanes] = ca * weight
            coarse[1, half * 8:half * 8 + 8, lanes] = sa * weight
        return carry

    lax.fori_loop(0, groups, factors, 0)

    width = 256

    def compute(j):
        def fill(i, carry):
            a = i // (chans // width)
            lanes = pl.ds(pl.multiple_of((i % (chans // width)) * width, width), width)
            out_rows = pl.ds(pl.multiple_of(a * FINE, FINE), FINE)
            ca = coarse[0, pl.ds(j * (COLS // FINE) + a, 1), lanes]
            sa = coarse[1, pl.ds(j * (COLS // FINE) + a, 1), lanes]
            cf = fine[0, :, lanes]
            sf = fine[1, :, lanes]
            table[p, out_rows, lanes] = (ca * cf - sa * sf).astype(jnp.bfloat16)
            table[1 - p, out_rows, lanes] = (sa * cf + ca * sf).astype(jnp.bfloat16)
            return carry

        lax.fori_loop(0, (COLS // FINE) * (chans // width), fill, 0)

        @pl.when(j == 0)
        def _():
            for xd in range(nx):
                local_copy(xd).wait()
                pol_copy(xd).wait()

        sign = 1.0 - 2.0 * p.astype(jnp.float32)
        dims = (((1,), (1,)), ((), ()))
        half_rows = nz * rows

        def half(i, carry):
            xd = lax.rem(1 - x + i + nx, nx)
            both = data[:, xd].reshape(2 * half_rows, chans)
            first = lax.dot_general(both, table[0], dims, preferred_element_type=jnp.float32)
            second = lax.dot_general(both, table[1], dims, preferred_element_type=jnp.float32)
            real = first[:half_rows] + second[half_rows:]
            imag = sign * (first[half_rows:] - second[:half_rows])

            @pl.when(i == 0)
            def _():
                xout[j, 0] = real.astype(jnp.bfloat16)
                xout[j, 1] = imag.astype(jnp.bfloat16)
                x_copy(j).start()

            @pl.when(i == 1)
            def _():
                sums[j, 0] = real
                sums[j, 1] = imag

            return carry

        lax.fori_loop(0, nx, half, 0)

    def total(j, d):
        return sums[j, :, pl.ds(pl.multiple_of(d * rows, rows), rows), :]

    def send(j, taken, slot, to, value):
        zout[j, taken] = value.astype(jnp.bfloat16)
        z_copy(j, taken, slot, to).start()

    def arrived(j, slot):
        z_copy(j, 0, slot, far_in).wait_recv()
        return zin[j, slot].astype(jnp.float32)

    def after_x(j):
        x_copy(j).wait_recv()
        sums[j] = sums[j] + xin[j].astype(jnp.float32)

        @pl.when(outer)
        def _():
            send(j, 0, 2, near_in, total(j, far_out))
            send(j, 1, 1, near_in, total(j, far_in))
            send(j, 2, 0, near_in, total(j, near_in))

        @pl.when(jnp.logical_not(outer))
        def _():
            send(j, 0, 0, near_out, total(j, near_out))

    def hop(j):
        @pl.when(jnp.logical_not(outer))
        def _():
            send(j, 1, 3, far_out, total(j, far_out) + arrived(j, 2))
            send(j, 2, 3, far_in, total(j, far_in) + arrived(j, 1))

    def finish(j):
        value = total(j, z) + arrived(j, 0) + arrived(j, 3)
        depth_id = j * COLS + lax.broadcasted_iota(jnp.int32, (rows, COLS), 1)
        inside = (depth_id >= NPHI // 2 - DEPTH_BLOCK * row_counts) & (
            depth_id < NPHI // 2 + DEPTH_BLOCK * row_counts)
        for part in range(2):
            columns = pl.ds(pl.multiple_of(part * NPHI + j * COLS, COLS), COLS)
            out_ref[:, columns] = jnp.where(inside, value[part], 0.0)

    owner = (z * nx + x) * 2 + p
    per_row = LANES // rows
    count_row = jnp.broadcast_to(count_ref[pl.ds(owner // per_row, 1), :], (rows, LANES))
    lane_id = lax.broadcasted_iota(jnp.int32, (rows, LANES), 1)
    own_lane = lax.broadcasted_iota(jnp.int32, (rows, LANES), 0) + lax.rem(owner, per_row) * rows
    row_counts = jnp.sum(jnp.where(lane_id == own_lane, count_row, 0), 1, keepdims=True)

    def stage(i, carry):
        @pl.when(i < PORTIONS)
        def _():
            compute(i)

        def late(lag, action):
            @pl.when((i >= lag) & (i < PORTIONS + lag))
            def _():
                action(i - lag)

        late(1, after_x)
        late(2, hop)
        late(3, finish)
        return carry

    lax.fori_loop(0, PORTIONS + 3, stage, 0)

    def drain(j, carry):
        x_copy(j).wait_send()
        for taken in range(3):
            z_copy(j, taken, 0, far_in).wait_send()
        return carry

    lax.fori_loop(0, PORTIONS, drain, 0)


def kernel_shards(nz, nx, stokes, lambda_sq, channel_flags, counts):
    beams = counts.shape[0]
    chans = stokes.shape[2]
    rows = beams // (nz * nx * 2)
    bf16, f32 = jnp.bfloat16, jnp.float32
    DMA = pltpu.SemaphoreType.DMA
    spectrum = pl.pallas_call(
        functools.partial(kernel, nz, nx, rows, chans),
        out_shape=jax.ShapeDtypeStruct((rows, 2 * NPHI), f32),
        in_specs=[pl.BlockSpec(memory_space=pl.ANY)] * 4,
        out_specs=pl.BlockSpec(memory_space=pltpu.VMEM),
        scratch_shapes=[
            pltpu.VMEM((lambda_sq.shape[0] // LANES, LANES), f32),
            pltpu.VMEM((lambda_sq.shape[0] // LANES, LANES), jnp.int32),
            pltpu.VMEM((beams // LANES, LANES), jnp.int32),
            pltpu.VMEM((2, nx, nz, rows, chans), bf16),
            pltpu.VMEM((2, FINE, chans), f32),
            pltpu.VMEM((2, COARSE, chans), f32),
            pltpu.VMEM((2, COLS, chans), bf16),
            pltpu.VMEM((PORTIONS, 2, nz * rows, COLS), f32),
            pltpu.VMEM((PORTIONS, 2, nz * rows, COLS), bf16),
            pltpu.VMEM((PORTIONS, 2, nz * rows, COLS), bf16),
            pltpu.VMEM((PORTIONS, 3, 2, rows, COLS), bf16),
            pltpu.VMEM((PORTIONS, 4, 2, rows, COLS), bf16),
            DMA((3,)), DMA((nx,)), DMA((nx,)), DMA((nx,)),
            DMA((PORTIONS,)), DMA((PORTIONS,)),
            DMA((PORTIONS, 3)), DMA((PORTIONS, 4)),
        ],
        compiler_params=pltpu.CompilerParams(
            collective_id=0, has_side_effects=True, vmem_limit_bytes=VMEM_BYTES),
        cost_estimate=pl.CostEstimate(
            flops=4 * beams * chans * NPHI, bytes_accessed=2 * beams * chans, transcendentals=0),
    )(
        stokes.reshape(nz, nx, 2, rows, chans),
        lambda_sq.reshape(-1, LANES),
        channel_flags.reshape(-1, LANES),
        counts.reshape(-1, LANES),
    )
    return spectrum


def solution(mesh):
    in_specs = (P("pol", "grp", ("beam", "slab")), P(), P(), P("grp"))
    out_specs = P(("grp", "beam", "slab", "pol"), None)
    nz, nx = mesh.shape["beam"], mesh.shape["slab"]
    if nx == 2 and nz == 4 and mesh.shape["pol"] == 2:
        body = functools.partial(kernel_shards, nz, nx)
    else:
        body = general_shards
    return jax.shard_map(body, mesh=mesh, in_specs=in_specs, out_specs=out_specs, check_vma=False)
```

```python
import functools
import math

import jax
import jax.numpy as jnp
from jax import lax
from jax.experimental import pallas as pl
from jax.experimental.pallas import tpu as pltpu
from jax.sharding import PartitionSpec as P

NPHI = 1024
DEPTH_BLOCK = 128
MESH = pl.DeviceIdType.MESH


depth_step = 32.0


def depth_values(depth_ids):
    return depth_step * (depth_ids.astype(jnp.float32) - NPHI // 2)


def build_table(lambda_block, flag_block, norm_scale, center, depths, first_pol):
    phases = (2.0 * depths)[None, :] * (lambda_block - center)[:, None]
    weight = (norm_scale * flag_block)[:, None]
    cos_part = weight * jnp.cos(phases)
    sin_part = weight * jnp.sin(phases)
    first_table = jnp.where(first_pol, cos_part, sin_part).astype(jnp.bfloat16)
    second_table = jnp.where(first_pol, -sin_part, cos_part).astype(jnp.bfloat16)
    return jnp.concatenate([first_table, second_table], 1)


def synth_dense(turned, lambda_local, flag_local, norm_scale, center, first_pol):
    row_count, chan_count = turned.shape
    block_width = min(1024, chan_count)
    block_count = chan_count // block_width
    depths = depth_values(jnp.arange(NPHI, dtype=jnp.int32))

    def add_block(index, totals):
        offset = index * block_width
        block = lax.dynamic_slice_in_dim(turned, offset, block_width, 1)
        lambda_block = lax.dynamic_slice_in_dim(lambda_local, offset, block_width, 0)
        flag_block = lax.dynamic_slice_in_dim(flag_local, offset, block_width, 0)
        phase_table = build_table(lambda_block, flag_block, norm_scale, center, depths, first_pol)
        return totals + jnp.dot(block, phase_table, preferred_element_type=jnp.float32)

    start_totals = jnp.zeros((row_count, 2 * NPHI), jnp.float32)
    return lax.fori_loop(0, block_count, add_block, start_totals)


def depth_mask(row_counts):
    depth_ids = jnp.arange(NPHI, dtype=jnp.int32)
    middle = NPHI // 2
    lower = middle - DEPTH_BLOCK * row_counts
    upper = middle + DEPTH_BLOCK * row_counts
    inside = (depth_ids[None, :] >= lower[:, None]) & (depth_ids[None, :] < upper[:, None])
    return jnp.concatenate([inside, inside], 1)


def general_shards(stokes, lambda_sq, channel_flags, counts):
    local_stokes = stokes[0]
    flag_float = channel_flags.astype(jnp.float32)
    flag_total = jnp.sum(flag_float)
    norm_scale = 1.0 / jnp.sqrt(flag_total)
    center = jnp.sum(flag_float * lambda_sq) / flag_total
    first_pol = lax.axis_index("pol") == 0
    beam_count = lax.axis_size("beam")
    slab_count = lax.axis_size("slab")
    total_beams = counts.shape[0]
    piece_index = lax.axis_index("beam")
    piece_rows = total_beams // beam_count
    turned = lax.all_to_all(local_stokes, "beam", split_axis=0, concat_axis=1, tiled=True)
    slab_index = lax.axis_index("slab")
    lambda_local = lax.dynamic_index_in_dim(
        lambda_sq.reshape(beam_count, slab_count, -1), slab_index, 1, keepdims=False
    ).reshape(-1)
    flag_local = lax.dynamic_index_in_dim(
        flag_float.reshape(beam_count, slab_count, -1), slab_index, 1, keepdims=False
    ).reshape(-1)
    row_counts = lax.dynamic_slice_in_dim(counts, piece_index * piece_rows, piece_rows, 0)
    partial_value = synth_dense(turned, lambda_local, flag_local, norm_scale, center, first_pol)
    partial_value = jnp.where(depth_mask(row_counts), partial_value, jnp.zeros_like(partial_value))
    return lax.psum_scatter(partial_value, ("slab", "pol"), scatter_dimension=0, tiled=True)


LANES = 128
PORTIONS = 4
COLS = NPHI // PORTIONS
SPLIT = 2
PIECES = PORTIONS * SPLIT
WIDE = COLS // SPLIT
FINE = 64
COARSE = NPHI // FINE

VMEM_BYTES = 60 * 2**20

HALF_TURN_HI = 3.140625
HALF_TURN_MID = 9.670257568359375e-04
HALF_TURN_LO = math.pi - HALF_TURN_HI - HALF_TURN_MID


def cos_sin(phase):
    turns = jnp.floor(phase * (1.0 / math.pi) + 0.5)
    rest = phase - turns * HALF_TURN_HI
    rest = rest - turns * HALF_TURN_MID
    rest = rest - turns * HALF_TURN_LO
    sign = 1.0 - 2.0 * (turns - 2.0 * jnp.floor(turns * 0.5))
    square = rest * rest
    cos_sum = jnp.full_like(square, 1.0 / math.factorial(12))
    for order in (10, 8, 6, 4, 2, 0):
        cos_sum = cos_sum * square + (-1.0) ** (order // 2) / math.factorial(order)
    sin_sum = jnp.full_like(square, -1.0 / math.factorial(11))
    for order in (9, 7, 5, 3, 1):
        sin_sum = sin_sum * square + (-1.0) ** (order // 2) / math.factorial(order)
    return sign * cos_sum, sign * rest * sin_sum


def kernel(nz, nx, rows, chans,
           stokes_ref, lam_hbm, flag_hbm, count_hbm, out_ref,
           lam_ref, flag_ref, count_ref,
           data, fine, coarse, table, sums, xout, xin, zout, zin,
           small_sem, local_sem, pol_send, pol_recv, x_send, x_recv, z_send, z_recv):
    z = lax.axis_index("beam")
    x = lax.axis_index("slab")
    p = lax.axis_index("pol")
    groups = chans // LANES

    side = z // 2
    outer = (z == 0) | (z == nz - 1)
    near_in, near_out = 1 + side, 3 * side
    far_in, far_out = 2 - side, 3 - 3 * side

    barrier = pltpu.get_barrier_semaphore()

    def greet(**device):
        pl.semaphore_signal(barrier, inc=1, device_id=device, device_id_type=MESH)

    greet(pol=1 - p)
    greet(slab=1 - x)
    greet(beam=far_in)

    @pl.when(outer)
    def _():
        greet(beam=near_in)

    @pl.when(jnp.logical_not(outer))
    def _():
        greet(beam=near_out)
        greet(beam=far_out)

    def local_copy(xd):
        return pltpu.make_async_copy(stokes_ref.at[:, xd, p], data.at[0, xd], local_sem.at[xd])

    def pol_copy(xd):
        return pltpu.make_async_remote_copy(
            src_ref=stokes_ref.at[:, xd, 1 - p], dst_ref=data.at[1, xd],
            send_sem=pol_send.at[xd], recv_sem=pol_recv.at[xd],
            device_id={"pol": 1 - p}, device_id_type=MESH)

    def x_copy(j):
        return pltpu.make_async_remote_copy(
            src_ref=xout.at[j], dst_ref=xin.at[j],
            send_sem=x_send.at[j], recv_sem=x_recv.at[j],
            device_id={"slab": 1 - x}, device_id_type=MESH)

    def z_copy(j, taken, slot, to):
        return pltpu.make_async_remote_copy(
            src_ref=zout.at[j, taken], dst_ref=zin.at[j, slot],
            send_sem=z_send.at[j, taken], recv_sem=z_recv.at[j, slot],
            device_id={"beam": to}, device_id_type=MESH)

    small = [pltpu.make_async_copy(source, held, small_sem.at[i]) for i, (source, held) in enumerate(
        [(lam_hbm, lam_ref), (flag_hbm, flag_ref), (count_hbm, count_ref)])]
    for copy in small:
        copy.start()
    for xd in (1 - x, x):
        local_copy(xd).start()

    @pl.when(outer)
    def _():
        pl.semaphore_wait(barrier, 4)

    @pl.when(jnp.logical_not(outer))
    def _():
        pl.semaphore_wait(barrier, 5)

    for xd in (1 - x, x):
        pol_copy(xd).start()

    for copy in small:
        copy.wait()
    flags = flag_ref[...].astype(jnp.float32)
    flag_total = jnp.sum(jnp.sum(flags, 0, keepdims=True), 1, keepdims=True)
    lam_total = jnp.sum(jnp.sum(flags * lam_ref[...], 0, keepdims=True), 1, keepdims=True)
    norm_scale = 1.0 / jnp.sqrt(flag_total)
    center = lam_total / flag_total
    first_group = (z * nx + x) * groups
    row_id = lax.broadcasted_iota(jnp.int32, (8, LANES), 0).astype(jnp.float32)
    step = 2.0 * depth_step

    def factors(g, carry):
        lanes = pl.ds(pl.multiple_of(g * LANES, LANES), LANES)
        offset = lam_ref[pl.ds(first_group + g, 1), :] - center
        weight = norm_scale * flag_ref[pl.ds(first_group + g, 1), :].astype(jnp.float32)
        cos_c, sin_c = cos_sin((step * row_id) * offset)
        cos_b, sin_b = cos_sin((step * 8.0 * row_id) * offset)
        for b in range(8):
            cb, sb = cos_b[b:b + 1, :], sin_b[b:b + 1, :]
            fine[0, b * 8:b * 8 + 8, lanes] = cb * cos_c - sb * sin_c
            fine[1, b * 8:b * 8 + 8, lanes] = sb * cos_c + cb * sin_c
        for half in range(COARSE // 8):
            ca, sa = cos_sin((step * FINE * (row_id + (8.0 * half - COARSE // 2))) * offset)
            coarse[0, half * 8:half * 8 + 8, lanes] = ca * weight
            coarse[1, half * 8:half * 8 + 8, lanes] = sa * weight
        return carry

    lax.fori_loop(0, groups, factors, 0)

    width = 256

    def compute(j):
        def fill(i, carry):
            a = i // (chans // width)
            lanes = pl.ds(pl.multiple_of((i % (chans // width)) * width, width), width)
            out_rows = pl.ds(pl.multiple_of(a * FINE, FINE), FINE)
            ca = coarse[0, pl.ds(j * (COLS // FINE) + a, 1), lanes]
            sa = coarse[1, pl.ds(j * (COLS // FINE) + a, 1), lanes]
            cf = fine[0, :, lanes]
            sf = fine[1, :, lanes]
            table[p, out_rows, lanes] = (ca * cf - sa * sf).astype(jnp.bfloat16)
            table[1 - p, out_rows, lanes] = (sa * cf + ca * sf).astype(jnp.bfloat16)
            return carry

        lax.fori_loop(0, (COLS // FINE) * (chans // width), fill, 0)
        sign = 1.0 - 2.0 * p.astype(jnp.float32)
        dims = (((1,), (1,)), ((), ()))
        half_rows = nz * rows

        def half(i, carry):
            xd = lax.rem(1 - x + i, nx)

            @pl.when(j == 0)
            def _():
                local_copy(xd).wait()
                pol_copy(xd).wait()

            both = data[:, xd].reshape(2 * half_rows, chans)
            first = lax.dot_general(both, table[0], dims, preferred_element_type=jnp.float32)
            second = lax.dot_general(both, table[1], dims, preferred_element_type=jnp.float32)
            real = first[:half_rows] + second[half_rows:]
            imag = sign * (first[half_rows:] - second[:half_rows])

            @pl.when(i == 0)
            def _():
                for h in range(SPLIT):
                    xout[j * SPLIT + h, 0] = real[:, h * WIDE:h * WIDE + WIDE].astype(jnp.bfloat16)
                    xout[j * SPLIT + h, 1] = imag[:, h * WIDE:h * WIDE + WIDE].astype(jnp.bfloat16)
                    x_copy(j * SPLIT + h).start()

            @pl.when(i == 1)
            def _():
                for h in range(SPLIT):
                    sums[j * SPLIT + h, 0] = real[:, h * WIDE:h * WIDE + WIDE]
                    sums[j * SPLIT + h, 1] = imag[:, h * WIDE:h * WIDE + WIDE]

            return carry

        lax.fori_loop(0, nx, half, 0)

    def total(j, d):
        return sums[j, :, pl.ds(pl.multiple_of(d * rows, rows), rows), :]

    def send(j, taken, slot, to, value):
        zout[j, taken] = value.astype(jnp.bfloat16)
        z_copy(j, taken, slot, to).start()

    def arrived(j, slot):
        z_copy(j, 0, slot, far_in).wait_recv()
        return zin[j, slot].astype(jnp.float32)

    def after_x(j):
        x_copy(j).wait_recv()
        sums[j] = sums[j] + xin[j].astype(jnp.float32)

        @pl.when(outer)
        def _():
            send(j, 0, 2, near_in, total(j, far_out))
            send(j, 1, 1, near_in, total(j, far_in))
            send(j, 2, 0, near_in, total(j, near_in))

        @pl.when(jnp.logical_not(outer))
        def _():
            send(j, 0, 0, near_out, total(j, near_out))

    def hop(j):
        @pl.when(jnp.logical_not(outer))
        def _():
            send(j, 1, 3, far_out, total(j, far_out) + arrived(j, 2))
            send(j, 2, 3, far_in, total(j, far_in) + arrived(j, 1))

    def finish(j):
        value = total(j, z) + arrived(j, 0) + arrived(j, 3)
        depth_id = j * WIDE + lax.broadcasted_iota(jnp.int32, (rows, WIDE), 1)
        inside = (depth_id >= NPHI // 2 - DEPTH_BLOCK * row_counts) & (
            depth_id < NPHI // 2 + DEPTH_BLOCK * row_counts)
        for part in range(2):
            columns = pl.ds(pl.multiple_of(part * NPHI + j * WIDE, WIDE), WIDE)
            out_ref[:, columns] = jnp.where(inside, value[part], 0.0)

    owner = (z * nx + x) * 2 + p
    per_row = LANES // rows
    count_row = jnp.broadcast_to(count_ref[pl.ds(owner // per_row, 1), :], (rows, LANES))
    lane_id = lax.broadcasted_iota(jnp.int32, (rows, LANES), 1)
    own_lane = lax.broadcasted_iota(jnp.int32, (rows, LANES), 0) + lax.rem(owner, per_row) * rows
    row_counts = jnp.sum(jnp.where(lane_id == own_lane, count_row, 0), 1, keepdims=True)

    def stage(i, carry):
        compute(i)

        @pl.when(i >= 2)
        def _():
            for h in range(SPLIT):
                after_x((i - 2) * SPLIT + h)

        @pl.when(i >= 3)
        def _():
            for h in range(SPLIT):
                hop((i - 3) * SPLIT + h)

        return carry

    lax.fori_loop(0, PORTIONS, stage, 0)

    for q in range((PORTIONS - 2) * SPLIT, PIECES):
        after_x(q)
        hop(q - SPLIT)
    for q in range(PIECES - 2 * SPLIT):
        finish(q)
    for q in range(PIECES - SPLIT, PIECES):
        hop(q)
        finish(q - SPLIT)
    for q in range(PIECES - SPLIT, PIECES):
        finish(q)

    def drain(j, carry):
        x_copy(j).wait_send()
        for taken in range(3):
            z_copy(j, taken, 0, far_in).wait_send()
        return carry

    lax.fori_loop(0, PIECES, drain, 0)


def kernel_shards(nz, nx, stokes, lambda_sq, channel_flags, counts):
    beams = counts.shape[0]
    chans = stokes.shape[2]
    rows = beams // (nz * nx * 2)
    bf16, f32 = jnp.bfloat16, jnp.float32
    DMA = pltpu.SemaphoreType.DMA
    spectrum = pl.pallas_call(
        functools.partial(kernel, nz, nx, rows, chans),
        out_shape=jax.ShapeDtypeStruct((rows, 2 * NPHI), f32),
        in_specs=[pl.BlockSpec(memory_space=pl.ANY)] * 4,
        out_specs=pl.BlockSpec(memory_space=pltpu.VMEM),
        scratch_shapes=[
            pltpu.VMEM((lambda_sq.shape[0] // LANES, LANES), f32),
            pltpu.VMEM((lambda_sq.shape[0] // LANES, LANES), jnp.int32),
            pltpu.VMEM((beams // LANES, LANES), jnp.int32),
            pltpu.VMEM((2, nx, nz, rows, chans), bf16),
            pltpu.VMEM((2, FINE, chans), f32),
            pltpu.VMEM((2, COARSE, chans), f32),
            pltpu.VMEM((2, COLS, chans), bf16),
            pltpu.VMEM((PIECES, 2, nz * rows, WIDE), f32),
            pltpu.VMEM((PIECES, 2, nz * rows, WIDE), bf16),
            pltpu.VMEM((PIECES, 2, nz * rows, WIDE), bf16),
            pltpu.VMEM((PIECES, 3, 2, rows, WIDE), bf16),
            pltpu.VMEM((PIECES, 4, 2, rows, WIDE), bf16),
            DMA((3,)), DMA((nx,)), DMA((nx,)), DMA((nx,)),
            DMA((PIECES,)), DMA((PIECES,)),
            DMA((PIECES, 3)), DMA((PIECES, 4)),
        ],
        compiler_params=pltpu.CompilerParams(
            collective_id=0, has_side_effects=True, vmem_limit_bytes=VMEM_BYTES),
        cost_estimate=pl.CostEstimate(
            flops=4 * beams * chans * NPHI, bytes_accessed=2 * beams * chans, transcendentals=0),
    )(
        stokes.reshape(nz, nx, 2, rows, chans),
        lambda_sq.reshape(-1, LANES),
        channel_flags.reshape(-1, LANES),
        counts.reshape(-1, LANES),
    )
    return spectrum


def solution(mesh):
    in_specs = (P("pol", "grp", ("beam", "slab")), P(), P(), P("grp"))
    out_specs = P(("grp", "beam", "slab", "pol"), None)
    nz, nx = mesh.shape["beam"], mesh.shape["slab"]
    if nx == 2 and nz == 4 and mesh.shape["pol"] == 2:
        body = functools.partial(kernel_shards, nz, nx)
    else:
        body = general_shards
    return jax.shard_map(body, mesh=mesh, in_specs=in_specs, out_specs=out_specs, check_vma=False)
```

```python
import functools
import math

import jax
import jax.numpy as jnp
from jax import lax
from jax.experimental import pallas as pl
from jax.experimental.pallas import tpu as pltpu
from jax.sharding import PartitionSpec as P

NPHI = 1024
DEPTH_BLOCK = 128
MESH = pl.DeviceIdType.MESH


depth_step = 32.0


def depth_values(depth_ids):
    return depth_step * (depth_ids.astype(jnp.float32) - NPHI // 2)


def build_table(lambda_block, flag_block, norm_scale, center, depths, first_pol):
    phases = (2.0 * depths)[None, :] * (lambda_block - center)[:, None]
    weight = (norm_scale * flag_block)[:, None]
    cos_part = weight * jnp.cos(phases)
    sin_part = weight * jnp.sin(phases)
    first_table = jnp.where(first_pol, cos_part, sin_part).astype(jnp.bfloat16)
    second_table = jnp.where(first_pol, -sin_part, cos_part).astype(jnp.bfloat16)
    return jnp.concatenate([first_table, second_table], 1)


def synth_dense(turned, lambda_local, flag_local, norm_scale, center, first_pol):
    row_count, chan_count = turned.shape
    block_width = min(1024, chan_count)
    block_count = chan_count // block_width
    depths = depth_values(jnp.arange(NPHI, dtype=jnp.int32))

    def add_block(index, totals):
        offset = index * block_width
        block = lax.dynamic_slice_in_dim(turned, offset, block_width, 1)
        lambda_block = lax.dynamic_slice_in_dim(lambda_local, offset, block_width, 0)
        flag_block = lax.dynamic_slice_in_dim(flag_local, offset, block_width, 0)
        phase_table = build_table(lambda_block, flag_block, norm_scale, center, depths, first_pol)
        return totals + jnp.dot(block, phase_table, preferred_element_type=jnp.float32)

    start_totals = jnp.zeros((row_count, 2 * NPHI), jnp.float32)
    return lax.fori_loop(0, block_count, add_block, start_totals)


def depth_mask(row_counts):
    depth_ids = jnp.arange(NPHI, dtype=jnp.int32)
    middle = NPHI // 2
    lower = middle - DEPTH_BLOCK * row_counts
    upper = middle + DEPTH_BLOCK * row_counts
    inside = (depth_ids[None, :] >= lower[:, None]) & (depth_ids[None, :] < upper[:, None])
    return jnp.concatenate([inside, inside], 1)


def general_shards(stokes, lambda_sq, channel_flags, counts):
    local_stokes = stokes[0]
    flag_float = channel_flags.astype(jnp.float32)
    flag_total = jnp.sum(flag_float)
    norm_scale = 1.0 / jnp.sqrt(flag_total)
    center = jnp.sum(flag_float * lambda_sq) / flag_total
    first_pol = lax.axis_index("pol") == 0
    beam_count = lax.axis_size("beam")
    slab_count = lax.axis_size("slab")
    total_beams = counts.shape[0]
    piece_index = lax.axis_index("beam")
    piece_rows = total_beams // beam_count
    turned = lax.all_to_all(local_stokes, "beam", split_axis=0, concat_axis=1, tiled=True)
    slab_index = lax.axis_index("slab")
    lambda_local = lax.dynamic_index_in_dim(
        lambda_sq.reshape(beam_count, slab_count, -1), slab_index, 1, keepdims=False
    ).reshape(-1)
    flag_local = lax.dynamic_index_in_dim(
        flag_float.reshape(beam_count, slab_count, -1), slab_index, 1, keepdims=False
    ).reshape(-1)
    row_counts = lax.dynamic_slice_in_dim(counts, piece_index * piece_rows, piece_rows, 0)
    partial_value = synth_dense(turned, lambda_local, flag_local, norm_scale, center, first_pol)
    partial_value = jnp.where(depth_mask(row_counts), partial_value, jnp.zeros_like(partial_value))
    return lax.psum_scatter(partial_value, ("slab", "pol"), scatter_dimension=0, tiled=True)


LANES = 128
PORTIONS = 4
COLS = NPHI // PORTIONS
SPLIT = 2
PIECES = PORTIONS * SPLIT
WIDE = COLS // SPLIT
TURNED = 5
FINE = 64
COARSE = NPHI // FINE

VMEM_BYTES = 60 * 2**20

HALF_TURN_HI = 3.140625
HALF_TURN_MID = 9.670257568359375e-04
HALF_TURN_LO = math.pi - HALF_TURN_HI - HALF_TURN_MID


def cos_sin(phase):
    turns = jnp.floor(phase * (1.0 / math.pi) + 0.5)
    rest = phase - turns * HALF_TURN_HI
    rest = rest - turns * HALF_TURN_MID
    rest = rest - turns * HALF_TURN_LO
    sign = 1.0 - 2.0 * (turns - 2.0 * jnp.floor(turns * 0.5))
    square = rest * rest
    cos_sum = jnp.full_like(square, 1.0 / math.factorial(12))
    for order in (10, 8, 6, 4, 2, 0):
        cos_sum = cos_sum * square + (-1.0) ** (order // 2) / math.factorial(order)
    sin_sum = jnp.full_like(square, -1.0 / math.factorial(11))
    for order in (9, 7, 5, 3, 1):
        sin_sum = sin_sum * square + (-1.0) ** (order // 2) / math.factorial(order)
    return sign * cos_sum, sign * rest * sin_sum


def kernel(nz, nx, rows, chans,
           stokes_ref, lam_hbm, flag_hbm, count_hbm, out_ref,
           lam_ref, flag_ref, count_ref,
           data, fine, coarse, table, sums, xout, xin, zout, zin,
           turned, turned_end, turned_xout, turned_xin, turned_zout, turned_zin,
           small_sem, local_sem, pol_send, pol_recv, x_send, x_recv, z_send, z_recv,
           turned_x_send, turned_x_recv, turned_z_send, turned_z_recv):
    z = lax.axis_index("beam")
    x = lax.axis_index("slab")
    p = lax.axis_index("pol")
    groups = chans // LANES

    side = z // 2
    outer = (z == 0) | (z == nz - 1)
    near_in, near_out = 1 + side, 3 * side
    far_in, far_out = 2 - side, 3 - 3 * side

    barrier = pltpu.get_barrier_semaphore()

    def greet(**device):
        pl.semaphore_signal(barrier, inc=1, device_id=device, device_id_type=MESH)

    greet(pol=1 - p)
    greet(slab=1 - x)
    greet(beam=far_in)

    @pl.when(outer)
    def _():
        greet(beam=near_in)

    @pl.when(jnp.logical_not(outer))
    def _():
        greet(beam=near_out)
        greet(beam=far_out)

    def local_copy(xd):
        return pltpu.make_async_copy(stokes_ref.at[:, xd, p], data.at[0, xd], local_sem.at[xd])

    def pol_copy(xd):
        return pltpu.make_async_remote_copy(
            src_ref=stokes_ref.at[:, xd, 1 - p], dst_ref=data.at[1, xd],
            send_sem=pol_send.at[xd], recv_sem=pol_recv.at[xd],
            device_id={"pol": 1 - p}, device_id_type=MESH)

    def x_copy(j):
        return pltpu.make_async_remote_copy(
            src_ref=xout.at[j], dst_ref=xin.at[j],
            send_sem=x_send.at[j], recv_sem=x_recv.at[j],
            device_id={"slab": 1 - x}, device_id_type=MESH)

    def z_copy(j, taken, slot, to):
        return pltpu.make_async_remote_copy(
            src_ref=zout.at[j, taken], dst_ref=zin.at[j, slot],
            send_sem=z_send.at[j, taken], recv_sem=z_recv.at[j, slot],
            device_id={"beam": to}, device_id_type=MESH)

    def turned_x_copy():
        return pltpu.make_async_remote_copy(
            src_ref=turned_xout, dst_ref=turned_xin, send_sem=turned_x_send, recv_sem=turned_x_recv,
            device_id={"slab": 1 - x}, device_id_type=MESH)

    def turned_z_copy(taken, slot, to):
        return pltpu.make_async_remote_copy(
            src_ref=turned_zout.at[taken], dst_ref=turned_zin.at[slot],
            send_sem=turned_z_send.at[taken], recv_sem=turned_z_recv.at[slot],
            device_id={"beam": to}, device_id_type=MESH)

    small = [pltpu.make_async_copy(source, held, small_sem.at[i]) for i, (source, held) in enumerate(
        [(lam_hbm, lam_ref), (flag_hbm, flag_ref), (count_hbm, count_ref)])]
    for copy in small:
        copy.start()
    for xd in (1 - x, x):
        local_copy(xd).start()

    @pl.when(outer)
    def _():
        pl.semaphore_wait(barrier, 4)

    @pl.when(jnp.logical_not(outer))
    def _():
        pl.semaphore_wait(barrier, 5)

    for xd in (1 - x, x):
        pol_copy(xd).start()

    for copy in small:
        copy.wait()
    flags = flag_ref[...].astype(jnp.float32)
    flag_total = jnp.sum(jnp.sum(flags, 0, keepdims=True), 1, keepdims=True)
    lam_total = jnp.sum(jnp.sum(flags * lam_ref[...], 0, keepdims=True), 1, keepdims=True)
    norm_scale = 1.0 / jnp.sqrt(flag_total)
    center = lam_total / flag_total
    first_group = (z * nx + x) * groups
    row_id = lax.broadcasted_iota(jnp.int32, (8, LANES), 0).astype(jnp.float32)
    step = 2.0 * depth_step

    def factors(g, carry):
        lanes = pl.ds(pl.multiple_of(g * LANES, LANES), LANES)
        offset = lam_ref[pl.ds(first_group + g, 1), :] - center
        weight = norm_scale * flag_ref[pl.ds(first_group + g, 1), :].astype(jnp.float32)
        cos_c, sin_c = cos_sin((step * row_id) * offset)
        cos_b, sin_b = cos_sin((step * 8.0 * row_id) * offset)
        for b in range(8):
            cb, sb = cos_b[b:b + 1, :], sin_b[b:b + 1, :]
            fine[0, b * 8:b * 8 + 8, lanes] = cb * cos_c - sb * sin_c
            fine[1, b * 8:b * 8 + 8, lanes] = sb * cos_c + cb * sin_c
        for half in range(COARSE // 8):
            ca, sa = cos_sin((step * FINE * (row_id + (8.0 * half - COARSE // 2))) * offset)
            coarse[0, half * 8:half * 8 + 8, lanes] = ca * weight
            coarse[1, half * 8:half * 8 + 8, lanes] = sa * weight
        return carry

    lax.fori_loop(0, groups, factors, 0)

    width = 256

    def compute(j):
        def fill(i, carry):
            a = i // (chans // width)
            lanes = pl.ds(pl.multiple_of((i % (chans // width)) * width, width), width)
            out_rows = pl.ds(pl.multiple_of(a * FINE, FINE), FINE)
            ca = coarse[0, pl.ds(j * (COLS // FINE) + a, 1), lanes]
            sa = coarse[1, pl.ds(j * (COLS // FINE) + a, 1), lanes]
            cf = fine[0, :, lanes]
            sf = fine[1, :, lanes]
            table[p, out_rows, lanes] = (ca * cf - sa * sf).astype(jnp.bfloat16)
            table[1 - p, out_rows, lanes] = (sa * cf + ca * sf).astype(jnp.bfloat16)
            return carry

        lax.fori_loop(0, (COLS // FINE) * (chans // width), fill, 0)
        sign = 1.0 - 2.0 * p.astype(jnp.float32)
        dims = (((1,), (1,)), ((), ()))
        half_rows = nz * rows

        def half(i, carry):
            xd = lax.rem(1 - x + i, nx)

            @pl.when(j == 0)
            def _():
                local_copy(xd).wait()
                pol_copy(xd).wait()

            both = data[:, xd].reshape(2 * half_rows, chans)
            first = lax.dot_general(both, table[0], dims, preferred_element_type=jnp.float32)
            second = lax.dot_general(both, table[1], dims, preferred_element_type=jnp.float32)
            real = first[:half_rows] + second[half_rows:]
            imag = sign * (first[half_rows:] - second[:half_rows])

            @pl.when(j == TURNED // SPLIT)
            def _():
                start = TURNED % SPLIT * WIDE
                turned[xd, 0] = real[:, start:start + WIDE]
                turned[xd, 1] = imag[:, start:start + WIDE]

            for h in range(SPLIT):
                @pl.when((i == 0) & (j * SPLIT + h != TURNED))
                def _():
                    xout[j * SPLIT + h, 0] = real[:, h * WIDE:h * WIDE + WIDE].astype(jnp.bfloat16)
                    xout[j * SPLIT + h, 1] = imag[:, h * WIDE:h * WIDE + WIDE].astype(jnp.bfloat16)
                    x_copy(j * SPLIT + h).start()

            @pl.when(i == 1)
            def _():
                for h in range(SPLIT):
                    sums[j * SPLIT + h, 0] = real[:, h * WIDE:h * WIDE + WIDE]
                    sums[j * SPLIT + h, 1] = imag[:, h * WIDE:h * WIDE + WIDE]

            return carry

        lax.fori_loop(0, nx, half, 0)

    def total(j, d):
        return sums[j, :, pl.ds(pl.multiple_of(d * rows, rows), rows), :]

    def send(j, taken, slot, to, value):
        zout[j, taken] = value.astype(jnp.bfloat16)
        z_copy(j, taken, slot, to).start()

    def arrived(j, slot):
        z_copy(j, 0, slot, far_in).wait_recv()
        return zin[j, slot].astype(jnp.float32)

    def after_x(j):
        x_copy(j).wait_recv()
        sums[j] = sums[j] + xin[j].astype(jnp.float32)

        @pl.when(outer)
        def _():
            send(j, 0, 2, near_in, total(j, far_out))
            send(j, 1, 1, near_in, total(j, far_in))
            send(j, 2, 0, near_in, total(j, near_in))

        @pl.when(jnp.logical_not(outer))
        def _():
            send(j, 0, 0, near_out, total(j, near_out))

    def hop(j):
        @pl.when(jnp.logical_not(outer))
        def _():
            send(j, 1, 3, far_out, total(j, far_out) + arrived(j, 2))
            send(j, 2, 3, far_in, total(j, far_in) + arrived(j, 1))

    def turned_total(d):
        return turned[:, :, pl.ds(pl.multiple_of(d * rows, rows), rows), :]

    def turned_send(taken, slot, to, value):
        turned_zout[taken] = value.astype(jnp.bfloat16)
        turned_z_copy(taken, slot, to).start()

    def turned_arrived(slot):
        turned_z_copy(0, slot, far_in).wait_recv()
        return turned_zin[slot].astype(jnp.float32)

    def turned_begin():
        @pl.when(outer)
        def _():
            turned_send(0, 2, near_in, turned_total(far_out))
            turned_send(1, 1, near_in, turned_total(far_in))
            turned_send(2, 0, near_in, turned_total(near_in))

        @pl.when(jnp.logical_not(outer))
        def _():
            turned_send(0, 0, near_out, turned_total(near_out))

    def turned_hop():
        @pl.when(jnp.logical_not(outer))
        def _():
            turned_send(1, 3, far_out, turned_total(far_out) + turned_arrived(2))
            turned_send(2, 3, far_in, turned_total(far_in) + turned_arrived(1))

    def turned_over_x():
        turned_end[...] = turned_total(z) + turned_arrived(0) + turned_arrived(3)
        turned_xout[...] = turned_end[1 - x].astype(jnp.bfloat16)
        turned_x_copy().start()

    def turned_finish():
        turned_x_copy().wait_recv()
        write(TURNED, turned_end[x] + turned_xin[...].astype(jnp.float32))

    def finish(j):
        write(j, total(j, z) + arrived(j, 0) + arrived(j, 3))

    def write(j, value):
        depth_id = j * WIDE + lax.broadcasted_iota(jnp.int32, (rows, WIDE), 1)
        inside = (depth_id >= NPHI // 2 - DEPTH_BLOCK * row_counts) & (
            depth_id < NPHI // 2 + DEPTH_BLOCK * row_counts)
        for part in range(2):
            columns = pl.ds(pl.multiple_of(part * NPHI + j * WIDE, WIDE), WIDE)
            out_ref[:, columns] = jnp.where(inside, value[part], 0.0)

    owner = (z * nx + x) * 2 + p
    per_row = LANES // rows
    count_row = jnp.broadcast_to(count_ref[pl.ds(owner // per_row, 1), :], (rows, LANES))
    lane_id = lax.broadcasted_iota(jnp.int32, (rows, LANES), 1)
    own_lane = lax.broadcasted_iota(jnp.int32, (rows, LANES), 0) + lax.rem(owner, per_row) * rows
    row_counts = jnp.sum(jnp.where(lane_id == own_lane, count_row, 0), 1, keepdims=True)

    def stage(i, carry):
        compute(i)

        @pl.when(i == 1)
        def _():
            after_x(0)

        @pl.when(i == 2)
        def _():
            after_x(1)
            turned_begin()
            hop(0)

        @pl.when(i == 3)
        def _():
            after_x(2)
            after_x(3)
            hop(1)

        return carry

    lax.fori_loop(0, PORTIONS, stage, 0)

    after_x(4)
    hop(2)
    turned_hop()
    hop(3)
    finish(0)
    after_x(6)
    finish(1)
    hop(4)
    turned_over_x()
    finish(2)
    after_x(7)
    finish(3)
    hop(6)
    finish(4)
    hop(7)
    turned_finish()
    finish(6)
    finish(7)

    def drain(j, carry):
        @pl.when(j != TURNED)
        def _():
            x_copy(j).wait_send()

        for taken in range(3):
            @pl.when(j != TURNED)
            def _():
                z_copy(j, taken, 0, far_in).wait_send()
        return carry

    lax.fori_loop(0, PIECES, drain, 0)
    turned_x_copy().wait_send()
    for taken in range(3):
        turned_z_copy(taken, 0, far_in).wait_send()


def kernel_shards(nz, nx, stokes, lambda_sq, channel_flags, counts):
    beams = counts.shape[0]
    chans = stokes.shape[2]
    rows = beams // (nz * nx * 2)
    bf16, f32 = jnp.bfloat16, jnp.float32
    DMA = pltpu.SemaphoreType.DMA
    spectrum = pl.pallas_call(
        functools.partial(kernel, nz, nx, rows, chans),
        out_shape=jax.ShapeDtypeStruct((rows, 2 * NPHI), f32),
        in_specs=[pl.BlockSpec(memory_space=pl.ANY)] * 4,
        out_specs=pl.BlockSpec(memory_space=pltpu.VMEM),
        scratch_shapes=[
            pltpu.VMEM((lambda_sq.shape[0] // LANES, LANES), f32),
            pltpu.VMEM((lambda_sq.shape[0] // LANES, LANES), jnp.int32),
            pltpu.VMEM((beams // LANES, LANES), jnp.int32),
            pltpu.VMEM((2, nx, nz, rows, chans), bf16),
            pltpu.VMEM((2, FINE, chans), f32),
            pltpu.VMEM((2, COARSE, chans), f32),
            pltpu.VMEM((2, COLS, chans), bf16),
            pltpu.VMEM((PIECES, 2, nz * rows, WIDE), f32),
            pltpu.VMEM((PIECES, 2, nz * rows, WIDE), bf16),
            pltpu.VMEM((PIECES, 2, nz * rows, WIDE), bf16),
            pltpu.VMEM((PIECES, 3, 2, rows, WIDE), bf16),
            pltpu.VMEM((PIECES, 4, 2, rows, WIDE), bf16),
            pltpu.VMEM((nx, 2, nz * rows, WIDE), f32),
            pltpu.VMEM((nx, 2, rows, WIDE), f32),
            pltpu.VMEM((2, rows, WIDE), bf16),
            pltpu.VMEM((2, rows, WIDE), bf16),
            pltpu.VMEM((3, nx, 2, rows, WIDE), bf16),
            pltpu.VMEM((4, nx, 2, rows, WIDE), bf16),
            DMA((3,)), DMA((nx,)), DMA((nx,)), DMA((nx,)),
            DMA((PIECES,)), DMA((PIECES,)),
            DMA((PIECES, 3)), DMA((PIECES, 4)),
            DMA, DMA, DMA((3,)), DMA((4,)),
        ],
        compiler_params=pltpu.CompilerParams(
            collective_id=0, has_side_effects=True, vmem_limit_bytes=VMEM_BYTES),
        cost_estimate=pl.CostEstimate(
            flops=4 * beams * chans * NPHI, bytes_accessed=2 * beams * chans, transcendentals=0),
    )(
        stokes.reshape(nz, nx, 2, rows, chans),
        lambda_sq.reshape(-1, LANES),
        channel_flags.reshape(-1, LANES),
        counts.reshape(-1, LANES),
    )
    return spectrum


def solution(mesh):
    in_specs = (P("pol", "grp", ("beam", "slab")), P(), P(), P("grp"))
    out_specs = P(("grp", "beam", "slab", "pol"), None)
    nz, nx = mesh.shape["beam"], mesh.shape["slab"]
    if nx == 2 and nz == 4 and mesh.shape["pol"] == 2:
        body = functools.partial(kernel_shards, nz, nx)
    else:
        body = general_shards
    return jax.shard_map(body, mesh=mesh, in_specs=in_specs, out_specs=out_specs, check_vma=False)
```

```python
import functools
import math

import jax
import jax.numpy as jnp
from jax import lax
from jax.experimental import pallas as pl
from jax.experimental.pallas import tpu as pltpu
from jax.sharding import PartitionSpec as P

NPHI = 1024
DEPTH_BLOCK = 128
MESH = pl.DeviceIdType.MESH


depth_step = 32.0


def depth_values(depth_ids):
    return depth_step * (depth_ids.astype(jnp.float32) - NPHI // 2)


def build_table(lambda_block, flag_block, norm_scale, center, depths, first_pol):
    phases = (2.0 * depths)[None, :] * (lambda_block - center)[:, None]
    weight = (norm_scale * flag_block)[:, None]
    cos_part = weight * jnp.cos(phases)
    sin_part = weight * jnp.sin(phases)
    first_table = jnp.where(first_pol, cos_part, sin_part).astype(jnp.bfloat16)
    second_table = jnp.where(first_pol, -sin_part, cos_part).astype(jnp.bfloat16)
    return jnp.concatenate([first_table, second_table], 1)


def synth_dense(turned, lambda_local, flag_local, norm_scale, center, first_pol):
    row_count, chan_count = turned.shape
    block_width = min(1024, chan_count)
    block_count = chan_count // block_width
    depths = depth_values(jnp.arange(NPHI, dtype=jnp.int32))

    def add_block(index, totals):
        offset = index * block_width
        block = lax.dynamic_slice_in_dim(turned, offset, block_width, 1)
        lambda_block = lax.dynamic_slice_in_dim(lambda_local, offset, block_width, 0)
        flag_block = lax.dynamic_slice_in_dim(flag_local, offset, block_width, 0)
        phase_table = build_table(lambda_block, flag_block, norm_scale, center, depths, first_pol)
        return totals + jnp.dot(block, phase_table, preferred_element_type=jnp.float32)

    start_totals = jnp.zeros((row_count, 2 * NPHI), jnp.float32)
    return lax.fori_loop(0, block_count, add_block, start_totals)


def depth_mask(row_counts):
    depth_ids = jnp.arange(NPHI, dtype=jnp.int32)
    middle = NPHI // 2
    lower = middle - DEPTH_BLOCK * row_counts
    upper = middle + DEPTH_BLOCK * row_counts
    inside = (depth_ids[None, :] >= lower[:, None]) & (depth_ids[None, :] < upper[:, None])
    return jnp.concatenate([inside, inside], 1)


def general_shards(stokes, lambda_sq, channel_flags, counts):
    local_stokes = stokes[0]
    flag_float = channel_flags.astype(jnp.float32)
    flag_total = jnp.sum(flag_float)
    norm_scale = 1.0 / jnp.sqrt(flag_total)
    center = jnp.sum(flag_float * lambda_sq) / flag_total
    first_pol = lax.axis_index("pol") == 0
    beam_count = lax.axis_size("beam")
    slab_count = lax.axis_size("slab")
    total_beams = counts.shape[0]
    piece_index = lax.axis_index("beam")
    piece_rows = total_beams // beam_count
    turned = lax.all_to_all(local_stokes, "beam", split_axis=0, concat_axis=1, tiled=True)
    slab_index = lax.axis_index("slab")
    lambda_local = lax.dynamic_index_in_dim(
        lambda_sq.reshape(beam_count, slab_count, -1), slab_index, 1, keepdims=False
    ).reshape(-1)
    flag_local = lax.dynamic_index_in_dim(
        flag_float.reshape(beam_count, slab_count, -1), slab_index, 1, keepdims=False
    ).reshape(-1)
    row_counts = lax.dynamic_slice_in_dim(counts, piece_index * piece_rows, piece_rows, 0)
    partial_value = synth_dense(turned, lambda_local, flag_local, norm_scale, center, first_pol)
    partial_value = jnp.where(depth_mask(row_counts), partial_value, jnp.zeros_like(partial_value))
    return lax.psum_scatter(partial_value, ("slab", "pol"), scatter_dimension=0, tiled=True)


LANES = 128
PORTIONS = 4
COLS = NPHI // PORTIONS
SPLIT = 2
PIECES = PORTIONS * SPLIT
WIDE = COLS // SPLIT
FINE = 64
COARSE = NPHI // FINE

VMEM_BYTES = 60 * 2**20

HALF_TURN_HI = 3.140625
HALF_TURN_MID = 9.670257568359375e-04
HALF_TURN_LO = math.pi - HALF_TURN_HI - HALF_TURN_MID


def cos_sin(phase):
    turns = jnp.floor(phase * (1.0 / math.pi) + 0.5)
    rest = phase - turns * HALF_TURN_HI
    rest = rest - turns * HALF_TURN_MID
    rest = rest - turns * HALF_TURN_LO
    sign = 1.0 - 2.0 * (turns - 2.0 * jnp.floor(turns * 0.5))
    square = rest * rest
    cos_sum = jnp.full_like(square, 1.0 / math.factorial(12))
    for order in (10, 8, 6, 4, 2, 0):
        cos_sum = cos_sum * square + (-1.0) ** (order // 2) / math.factorial(order)
    sin_sum = jnp.full_like(square, -1.0 / math.factorial(11))
    for order in (9, 7, 5, 3, 1):
        sin_sum = sin_sum * square + (-1.0) ** (order // 2) / math.factorial(order)
    return sign * cos_sum, sign * rest * sin_sum


def kernel(nz, nx, rows, chans,
           stokes_ref, lam_hbm, flag_hbm, count_hbm, out_ref,
           lam_ref, flag_ref, count_ref,
           data, fine, coarse, table, sums, xout, xin, zout, zin,
           small_sem, local_sem, pol_send, pol_recv, x_send, x_recv, z_send, z_recv):
    z = lax.axis_index("beam")
    x = lax.axis_index("slab")
    p = lax.axis_index("pol")
    groups = chans // LANES

    side = z // 2
    outer = (z == 0) | (z == nz - 1)
    near_in, near_out = 1 + side, 3 * side
    far_in, far_out = 2 - side, 3 - 3 * side

    barrier = pltpu.get_barrier_semaphore()

    def greet(**device):
        pl.semaphore_signal(barrier, inc=1, device_id=device, device_id_type=MESH)

    greet(pol=1 - p)
    greet(slab=1 - x)
    greet(beam=far_in)

    @pl.when(outer)
    def _():
        greet(beam=near_in)

    @pl.when(jnp.logical_not(outer))
    def _():
        greet(beam=near_out)
        greet(beam=far_out)

    def local_copy(xd):
        return pltpu.make_async_copy(stokes_ref.at[:, xd, p], data.at[0, xd], local_sem.at[xd])

    def pol_copy(xd):
        return pltpu.make_async_remote_copy(
            src_ref=stokes_ref.at[:, xd, 1 - p], dst_ref=data.at[1, xd],
            send_sem=pol_send.at[xd], recv_sem=pol_recv.at[xd],
            device_id={"pol": 1 - p}, device_id_type=MESH)

    def x_copy(j):
        return pltpu.make_async_remote_copy(
            src_ref=xout.at[j], dst_ref=xin.at[j],
            send_sem=x_send.at[j], recv_sem=x_recv.at[j],
            device_id={"slab": 1 - x}, device_id_type=MESH)

    def z_copy(j, taken, slot, to):
        return pltpu.make_async_remote_copy(
            src_ref=zout.at[j, taken], dst_ref=zin.at[j, slot],
            send_sem=z_send.at[j, taken], recv_sem=z_recv.at[j, slot],
            device_id={"beam": to}, device_id_type=MESH)

    def z_copy_all(j):
        return pltpu.make_async_remote_copy(
            src_ref=zout.at[j], dst_ref=zin.at[j, pl.ds(0, 3)],
            send_sem=z_send.at[j, 0], recv_sem=z_recv.at[j, 0],
            device_id={"beam": near_in}, device_id_type=MESH)

    small = [pltpu.make_async_copy(source, held, small_sem.at[i]) for i, (source, held) in enumerate(
        [(lam_hbm, lam_ref), (flag_hbm, flag_ref), (count_hbm, count_ref)])]
    for copy in small:
        copy.start()
    for xd in (1 - x, x):
        local_copy(xd).start()

    @pl.when(outer)
    def _():
        pl.semaphore_wait(barrier, 4)

    @pl.when(jnp.logical_not(outer))
    def _():
        pl.semaphore_wait(barrier, 5)

    for xd in (1 - x, x):
        pol_copy(xd).start()

    for copy in small:
        copy.wait()
    flags = flag_ref[...].astype(jnp.float32)
    flag_total = jnp.sum(jnp.sum(flags, 0, keepdims=True), 1, keepdims=True)
    lam_total = jnp.sum(jnp.sum(flags * lam_ref[...], 0, keepdims=True), 1, keepdims=True)
    norm_scale = 1.0 / jnp.sqrt(flag_total)
    center = lam_total / flag_total
    first_group = (z * nx + x) * groups
    row_id = lax.broadcasted_iota(jnp.int32, (8, LANES), 0).astype(jnp.float32)
    step = 2.0 * depth_step

    def factors(g, carry):
        lanes = pl.ds(pl.multiple_of(g * LANES, LANES), LANES)
        offset = lam_ref[pl.ds(first_group + g, 1), :] - center
        weight = norm_scale * flag_ref[pl.ds(first_group + g, 1), :].astype(jnp.float32)
        cos_c, sin_c = cos_sin((step * row_id) * offset)
        cos_b, sin_b = cos_sin((step * 8.0 * row_id) * offset)
        for b in range(8):
            cb, sb = cos_b[b:b + 1, :], sin_b[b:b + 1, :]
            fine[0, b * 8:b * 8 + 8, lanes] = cb * cos_c - sb * sin_c
            fine[1, b * 8:b * 8 + 8, lanes] = sb * cos_c + cb * sin_c
        for half in range(COARSE // 8):
            ca, sa = cos_sin((step * FINE * (row_id + (8.0 * half - COARSE // 2))) * offset)
            coarse[0, half * 8:half * 8 + 8, lanes] = ca * weight
            coarse[1, half * 8:half * 8 + 8, lanes] = sa * weight
        return carry

    lax.fori_loop(0, groups, factors, 0)

    width = 256

    def compute(j):
        def fill(i, carry):
            a = i // (chans // width)
            lanes = pl.ds(pl.multiple_of((i % (chans // width)) * width, width), width)
            out_rows = pl.ds(pl.multiple_of(a * FINE, FINE), FINE)
            ca = coarse[0, pl.ds(j * (COLS // FINE) + a, 1), lanes]
            sa = coarse[1, pl.ds(j * (COLS // FINE) + a, 1), lanes]
            cf = fine[0, :, lanes]
            sf = fine[1, :, lanes]
            table[p, out_rows, lanes] = (ca * cf - sa * sf).astype(jnp.bfloat16)
            table[1 - p, out_rows, lanes] = (sa * cf + ca * sf).astype(jnp.bfloat16)
            return carry

        lax.fori_loop(0, (COLS // FINE) * (chans // width), fill, 0)
        sign = 1.0 - 2.0 * p.astype(jnp.float32)
        dims = (((1,), (1,)), ((), ()))
        half_rows = nz * rows

        def half(i, carry):
            xd = lax.rem(1 - x + i, nx)

            @pl.when(j == 0)
            def _():
                local_copy(xd).wait()
                pol_copy(xd).wait()

            both = data[:, xd].reshape(2 * half_rows, chans)
            first = lax.dot_general(both, table[0], dims, preferred_element_type=jnp.float32)
            second = lax.dot_general(both, table[1], dims, preferred_element_type=jnp.float32)
            real = first[:half_rows] + second[half_rows:]
            imag = sign * (first[half_rows:] - second[:half_rows])

            @pl.when(i == 0)
            def _():
                for h in range(SPLIT):
                    xout[j * SPLIT + h, 0] = real[:, h * WIDE:h * WIDE + WIDE].astype(jnp.bfloat16)
                    xout[j * SPLIT + h, 1] = imag[:, h * WIDE:h * WIDE + WIDE].astype(jnp.bfloat16)
                    x_copy(j * SPLIT + h).start()

            @pl.when(i == 1)
            def _():
                for h in range(SPLIT):
                    sums[j * SPLIT + h, 0] = real[:, h * WIDE:h * WIDE + WIDE]
                    sums[j * SPLIT + h, 1] = imag[:, h * WIDE:h * WIDE + WIDE]

            return carry

        lax.fori_loop(0, nx, half, 0)

    def total(j, d):
        return sums[j, :, pl.ds(pl.multiple_of(d * rows, rows), rows), :]

    def send(j, taken, slot, to, value):
        zout[j, taken] = value.astype(jnp.bfloat16)
        z_copy(j, taken, slot, to).start()

    def arrived(j, slot):
        z_copy(j, 0, slot, far_in).wait_recv()
        return zin[j, slot].astype(jnp.float32)

    def after_x(j):
        x_copy(j).wait_recv()
        sums[j] = sums[j] + xin[j].astype(jnp.float32)

        @pl.when(outer)
        def _():
            zout[j, 0] = total(j, near_in).astype(jnp.bfloat16)
            zout[j, 1] = total(j, far_in).astype(jnp.bfloat16)
            zout[j, 2] = total(j, far_out).astype(jnp.bfloat16)
            z_copy_all(j).start()

        @pl.when(jnp.logical_not(outer))
        def _():
            send(j, 0, 0, near_out, total(j, near_out))

    def hop(j):
        @pl.when(jnp.logical_not(outer))
        def _():
            z_copy_all(j).wait_recv()
            send(j, 1, 3, far_out, total(j, far_out) + zin[j, 2].astype(jnp.float32))
            send(j, 2, 3, far_in, total(j, far_in) + zin[j, 1].astype(jnp.float32))

    def finish(j):
        @pl.when(outer)
        def _():
            z_copy(j, 0, 0, far_in).wait_recv()

        value = total(j, z) + zin[j, 0].astype(jnp.float32) + arrived(j, 3)
        depth_id = j * WIDE + lax.broadcasted_iota(jnp.int32, (rows, WIDE), 1)
        inside = (depth_id >= NPHI // 2 - DEPTH_BLOCK * row_counts) & (
            depth_id < NPHI // 2 + DEPTH_BLOCK * row_counts)
        for part in range(2):
            columns = pl.ds(pl.multiple_of(part * NPHI + j * WIDE, WIDE), WIDE)
            out_ref[:, columns] = jnp.where(inside, value[part], 0.0)

    owner = (z * nx + x) * 2 + p
    per_row = LANES // rows
    count_row = jnp.broadcast_to(count_ref[pl.ds(owner // per_row, 1), :], (rows, LANES))
    lane_id = lax.broadcasted_iota(jnp.int32, (rows, LANES), 1)
    own_lane = lax.broadcasted_iota(jnp.int32, (rows, LANES), 0) + lax.rem(owner, per_row) * rows
    row_counts = jnp.sum(jnp.where(lane_id == own_lane, count_row, 0), 1, keepdims=True)

    def stage(i, carry):
        compute(i)

        @pl.when(i >= 2)
        def _():
            for h in range(SPLIT):
                after_x((i - 2) * SPLIT + h)

        @pl.when(i >= 3)
        def _():
            for h in range(SPLIT):
                hop((i - 3) * SPLIT + h)

        return carry

    lax.fori_loop(0, PORTIONS, stage, 0)

    for q in range((PORTIONS - 2) * SPLIT, PIECES):
        after_x(q)
        hop(q - SPLIT)
    for q in range(PIECES - 2 * SPLIT):
        finish(q)
    for q in range(PIECES - SPLIT, PIECES):
        hop(q)
        finish(q - SPLIT)
    for q in range(PIECES - SPLIT, PIECES):
        finish(q)

    def drain(j, carry):
        x_copy(j).wait_send()

        @pl.when(outer)
        def _():
            z_copy_all(j).wait_send()

        @pl.when(jnp.logical_not(outer))
        def _():
            for taken in range(3):
                z_copy(j, taken, 0, far_in).wait_send()
        return carry

    lax.fori_loop(0, PIECES, drain, 0)


def kernel_shards(nz, nx, stokes, lambda_sq, channel_flags, counts):
    beams = counts.shape[0]
    chans = stokes.shape[2]
    rows = beams // (nz * nx * 2)
    bf16, f32 = jnp.bfloat16, jnp.float32
    DMA = pltpu.SemaphoreType.DMA
    spectrum = pl.pallas_call(
        functools.partial(kernel, nz, nx, rows, chans),
        out_shape=jax.ShapeDtypeStruct((rows, 2 * NPHI), f32),
        in_specs=[pl.BlockSpec(memory_space=pl.ANY)] * 4,
        out_specs=pl.BlockSpec(memory_space=pltpu.VMEM),
        scratch_shapes=[
            pltpu.VMEM((lambda_sq.shape[0] // LANES, LANES), f32),
            pltpu.VMEM((lambda_sq.shape[0] // LANES, LANES), jnp.int32),
            pltpu.VMEM((beams // LANES, LANES), jnp.int32),
            pltpu.VMEM((2, nx, nz, rows, chans), bf16),
            pltpu.VMEM((2, FINE, chans), f32),
            pltpu.VMEM((2, COARSE, chans), f32),
            pltpu.VMEM((2, COLS, chans), bf16),
            pltpu.VMEM((PIECES, 2, nz * rows, WIDE), f32),
            pltpu.VMEM((PIECES, 2, nz * rows, WIDE), bf16),
            pltpu.VMEM((PIECES, 2, nz * rows, WIDE), bf16),
            pltpu.VMEM((PIECES, 3, 2, rows, WIDE), bf16),
            pltpu.VMEM((PIECES, 4, 2, rows, WIDE), bf16),
            DMA((3,)), DMA((nx,)), DMA((nx,)), DMA((nx,)),
            DMA((PIECES,)), DMA((PIECES,)),
            DMA((PIECES, 3)), DMA((PIECES, 4)),
        ],
        compiler_params=pltpu.CompilerParams(
            collective_id=0, has_side_effects=True, vmem_limit_bytes=VMEM_BYTES),
        cost_estimate=pl.CostEstimate(
            flops=4 * beams * chans * NPHI, bytes_accessed=2 * beams * chans, transcendentals=0),
    )(
        stokes.reshape(nz, nx, 2, rows, chans),
        lambda_sq.reshape(-1, LANES),
        channel_flags.reshape(-1, LANES),
        counts.reshape(-1, LANES),
    )
    return spectrum


def solution(mesh):
    in_specs = (P("pol", "grp", ("beam", "slab")), P(), P(), P("grp"))
    out_specs = P(("grp", "beam", "slab", "pol"), None)
    nz, nx = mesh.shape["beam"], mesh.shape["slab"]
    if nx == 2 and nz == 4 and mesh.shape["pol"] == 2:
        body = functools.partial(kernel_shards, nz, nx)
    else:
        body = general_shards
    return jax.shard_map(body, mesh=mesh, in_specs=in_specs, out_specs=out_specs, check_vma=False)
```
